32 devices in a mesh: ctx: 16 (over z, x, core), tp: 2 (over y).
Axes of the slice: x: 2, y: 2, z: 4, core: 2. Of those that a mesh axis runs over, the one named last changes fastest.
Arguments:
- features: bfloat16 [8192, 3, 4096], P('ctx', None, 'tp'), may hold values from -6 to 6
- short_filter: float32 [3, 7, 4096], P(None, None, 'tp'), may hold values from -2 to 2
- decay_rate: float32 [16, 4096], P(None, 'tp'), may hold values from 0 to 1, as said below
- residue: float32 [16, 4096], P(None, 'tp'), may hold values from -2 to 2
- skip_gain: float32 [4096], P('tp'), may hold values from -4 to 4
- norm_gain: float32 [4096], replicated, may hold values from 0.1 to 1.9
- qkv_weight: bfloat16 [4096, 3, 2048], P('ctx', None, 'tp'), may hold values from -2 to 2
Outputs:
- mixer: bfloat16 [8192, 4096], P('ctx', 'tp')
- attended: bfloat16 [8192, 2048], P('ctx', 'tp')
The draws below stay inside these ranges and needn't reach their ends.
Inputs may be any that keep to these rules, and one draw needn't show every extreme that they name: `decay_rate`: decay rates are positive.
All inputs are finite; a program needn't handle non-finite values.
Results may differ from the reference program's by a relative error of at most 0.01.
Values may be sent and summed in bfloat16 or wider, within the bound.
A program may use at most 192 MiB of HBM per device.

```python
import math
import jax
import jax.numpy as jnp
from jax import lax

D = 4096
HD = 128
HEADS = 16
NMODES = 16
TAPS = 7
WINDOW = 3
TOK_DEV = 512
TOKENS = 8192
N_CTX = 16


def draw_decay_rate(key, part):
    lowest = math.log(0.1 / TOKENS)
    highest = math.log(1.0 / 30.0)
    unit = jax.random.uniform(jax.random.fold_in(key, 11), (NMODES, D), jnp.float32)
    return jnp.exp(lowest + unit * (highest - lowest))


def draw_qkv_weight(key, part):
    base = jax.random.truncated_normal(jax.random.fold_in(key, 21), -4.0, 4.0, (D, 3, HEADS, HD), jnp.float32) * D ** (-0.5)
    return base.reshape(D, 3, HEADS * HD).astype(jnp.bfloat16)


def level_of(own_key, shape, cuts, low, high):
    level, own = 1.0, jax.random.fold_in(own_key, 6)
    for axis_at, shards_of in cuts:
        draws = jnp.exp(jax.random.uniform(jax.random.fold_in(own, axis_at), (shards_of,), jnp.float32, low / len(cuts), high / len(cuts)))
        level = level * jnp.repeat(draws, shape[axis_at] // shards_of).reshape([-1 if axis == axis_at else 1 for axis in range(len(shape))])
    return level


def centred(stream_key, dims, spread, bound, split=(), kind=jnp.bfloat16):
    values = spread * jax.random.normal(stream_key, dims, jnp.float32)
    if split:
        values = values * level_of(stream_key, dims, split, -0.22, 0.18)
    return jnp.clip(values, -bound, bound).astype(kind)


def setup_inputs(seed: int = 0) -> dict:
    key_of = jax.random.split(jax.random.key(seed), 8)
    features = centred(key_of[0], (TOKENS, 3, D), 1.0, 6.0, ((0, 16), (2, 2)))
    short_filter = centred(key_of[1], (3, TAPS, D), TAPS ** -0.5, 2.0, ((2, 2),), jnp.float32)
    decay_rate = draw_decay_rate(jax.random.fold_in(key_of[7], 71), 0)
    residue = centred(key_of[3], (NMODES, D), 0.35, 2.0, ((1, 2),), jnp.float32)
    skip_gain = centred(key_of[4], (D,), 1.0, 4.0, ((0, 2),), jnp.float32)
    norm_gain = jnp.clip(1.0 + 0.18 * jax.random.normal(key_of[5], (D,), jnp.float32), 0.1, 1.9)
    qkv_weight = draw_qkv_weight(jax.random.fold_in(key_of[7], 71), 0)
    return dict(features=features, short_filter=short_filter, decay_rate=decay_rate, residue=residue, skip_gain=skip_gain, norm_gain=norm_gain, qkv_weight=qkv_weight)


EPSILON = 1e-06

def hyena_group(feat_group, taps_group, decay_group, residue_group, skip_group):
    as_float = feat_group.astype(jnp.float32)
    padded = jnp.pad(as_float, ((TAPS - 1, 0), (0, 0), (0, 0)))
    short = jnp.zeros_like(as_float)
    for offset in range(TAPS):
        first_row = TAPS - 1 - offset
        short = short + taps_group[:, offset, :][None] * padded[first_row:first_row + TOKENS]
    gated = lax.optimization_barrier((short[:, 1] * short[:, 2]).astype(jnp.bfloat16)).astype(jnp.float32)
    channels = feat_group.shape[2]
    lag_values = jnp.arange(TOKENS).astype(jnp.float32)
    kernel = jnp.zeros((channels, TOKENS), jnp.float32)
    for mode in range(NMODES):
        mode_weight = residue_group[mode] * jnp.sqrt(decay_group[mode])
        kernel = kernel + mode_weight[:, None] * jnp.exp(-decay_group[mode][:, None] * lag_values[None, :])
    length = 2 * TOKENS
    spectrum = jnp.fft.rfft(gated.T, n=length) * jnp.fft.rfft(kernel, n=length)
    filtered = jnp.fft.irfft(spectrum, n=length)[:, :TOKENS].T + skip_group[None] * gated
    filtered = lax.optimization_barrier(filtered.astype(jnp.bfloat16)).astype(jnp.float32)
    return (short[:, 0] * filtered).astype(jnp.bfloat16)

def reference(features, short_filter, decay_rate, residue, skip_gain, norm_gain, qkv_weight):
    group = 128 if D % 128 == 0 else D
    count = D // group
    feats = features.reshape(TOKENS, 3, count, group).transpose(2, 0, 1, 3)
    taps = short_filter.reshape(3, TAPS, count, group).transpose(2, 0, 1, 3)
    decays = decay_rate.reshape(NMODES, count, group).transpose(1, 0, 2)
    residues = residue.reshape(NMODES, count, group).transpose(1, 0, 2)
    skips = skip_gain.reshape(count, group)
    pieces = lax.map(lambda items: hyena_group(*items), (feats, taps, decays, residues, skips))
    mixer = pieces.transpose(1, 0, 2).reshape(TOKENS, D)
    head_cols = HEADS * HD
    weight_flat = qkv_weight.reshape(D, 3 * head_cols)

    def project(block):
        as_float = block.astype(jnp.float32)
        inverse = lax.rsqrt(lax.optimization_barrier(jnp.mean(as_float * as_float, axis=1, keepdims=True)) + EPSILON)
        normed = (as_float * inverse * norm_gain[None]).astype(jnp.bfloat16)
        return jnp.dot(normed, weight_flat, preferred_element_type=jnp.float32).astype(jnp.bfloat16)
    projected = lax.map(project, mixer.reshape(N_CTX, TOK_DEV, D))
    projected = projected.reshape(TOKENS, 3, HEADS, HD)
    queries = projected[:, 0].reshape(N_CTX, TOK_DEV, HEADS, HD)
    key_values = jnp.pad(projected[:, 1:3], (((WINDOW - 1) * TOK_DEV, 0), (0, 0), (0, 0), (0, 0)))

    def attend(items):
        index, query = items
        first_row = (index * TOK_DEV).astype(jnp.int32)
        window_kv = lax.dynamic_slice_in_dim(key_values, first_row, WINDOW * TOK_DEV, 0)
        keys = window_kv[:, 0].astype(jnp.float32)
        values = window_kv[:, 1].astype(jnp.float32)
        query_pos = index * TOK_DEV + jnp.arange(TOK_DEV, dtype=jnp.int32)
        key_pos = index * TOK_DEV - (WINDOW - 1) * TOK_DEV + jnp.arange(WINDOW * TOK_DEV, dtype=jnp.int32)
        allowed = (key_pos[None, :] >= 0) & (key_pos[None, :] <= query_pos[:, None])
        scores = jnp.einsum('thd,shd->hts', query.astype(jnp.float32), keys) / math.sqrt(HD)
        scores = jnp.where(allowed[None], scores, -jnp.inf)
        peak = lax.optimization_barrier(jnp.max(scores, axis=2, keepdims=True))
        expo = jnp.exp(scores - peak)
        total = lax.optimization_barrier(jnp.sum(expo, axis=2))
        rounded = lax.optimization_barrier(expo.astype(jnp.bfloat16)).astype(jnp.float32)
        output = jnp.einsum('hts,shd->thd', rounded, values) / total.T[:, :, None]
        return output.astype(jnp.bfloat16).reshape(TOK_DEV, head_cols)
    attended = lax.map(attend, (jnp.arange(N_CTX, dtype=jnp.int32), queries))
    return (mixer, attended.reshape(TOKENS, head_cols))
```

```python
import functools
import math

import jax
import jax.numpy as jnp
from jax import lax
from jax.experimental import pallas as pl
from jax.experimental.pallas import tpu as pltpu
from jax.sharding import PartitionSpec as P

HD = 128
TAPS = 7
WINDOW = 3
EPSILON = 1e-06
LANES = 128
SEGMENTS = 8
HALO = 16
RADIX = 4
MIB = 1 << 20


def shifted(value, axis, steps):
    count = lax.axis_size(axis)
    return lax.ppermute(value, axis, [(source, source + steps) for source in range(count - steps)])


def mode_rows(values, modes):
    return [jnp.broadcast_to(values[n : n + 1], (SEGMENTS, LANES)) for n in range(modes)]


def short_kernel(feat_ref, halo_ref, taps_ref, decay_ref, gated_ref, first_ref, enter_ref, end_ref, ext, gs, ends):
    tokens = feat_ref.shape[1]
    seg = tokens // SEGMENTS
    modes = decay_ref.shape[0]
    streams = []
    for j in range(3):
        ext[j, :HALO] = halo_ref[j].astype(jnp.float32)
        ext[j, HALO:] = feat_ref[j].astype(jnp.float32)
        total = taps_ref[j, 0:1] * ext[j, HALO:]
        for i in range(1, TAPS):
            total = total + taps_ref[j, i : i + 1] * ext[j, HALO - i : HALO - i + tokens]
        if j == 0:
            first_ref[...] = total
        elif j == 1:
            gs[...] = total
        else:
            gated = (gs[...] * total).astype(jnp.bfloat16)
    gated_ref[...] = gated
    gs[...] = gated.astype(jnp.float32)
    rate = decay_ref[...]
    decays = mode_rows(jnp.exp(-rate), modes)

    def step(t, states):
        g = gs[pl.ds(t, SEGMENTS, stride=seg), :]
        return tuple(a * s + g for a, s in zip(decays, states))

    zero = jnp.zeros((SEGMENTS, LANES), jnp.float32)
    states = lax.fori_loop(0, seg, step, (zero,) * modes, unroll=8)
    for n in range(modes):
        ends[n * SEGMENTS : (n + 1) * SEGMENTS] = states[n]
    across = jnp.exp(-float(seg) * rate)
    entering = jnp.zeros((modes, LANES), jnp.float32)
    for j in range(SEGMENTS):
        enter_ref[j] = entering
        entering = across * entering + ends[pl.ds(j, modes, stride=SEGMENTS), :]
    end_ref[...] = entering


def long_kernel(gated_ref, first_ref, enter_ref, state_ref, decay_ref, residue_ref, skip_ref, mixer_ref, gs, ys, starts):
    tokens = gated_ref.shape[0]
    seg = tokens // SEGMENTS
    modes = decay_ref.shape[0]
    rate = decay_ref[...]
    gs[...] = gated_ref[...].astype(jnp.float32)
    for j in range(SEGMENTS):
        starts[j * modes : (j + 1) * modes] = enter_ref[j] + jnp.exp(-float(j * seg) * rate) * state_ref[...]
    decays = mode_rows(jnp.exp(-rate), modes)
    weights = mode_rows(residue_ref[...] * jnp.sqrt(rate), modes)
    skip = jnp.broadcast_to(skip_ref[...], (SEGMENTS, LANES))

    def step(t, states):
        g = gs[pl.ds(t, SEGMENTS, stride=seg), :]
        states = tuple(a * s + g for a, s in zip(decays, states))
        terms = [w * s for w, s in zip(weights, states)]
        while len(terms) > 1:
            terms = [sum(terms[i : i + 2]) for i in range(0, len(terms), 2)]
        ys[pl.ds(t, SEGMENTS, stride=seg), :] = terms[0] + skip * g
        return states

    first = tuple(starts[pl.ds(n, SEGMENTS, stride=modes), :] for n in range(modes))
    lax.fori_loop(0, seg, step, first, unroll=8)
    filtered = ys[...].astype(jnp.bfloat16).astype(jnp.float32)
    mixer_ref[...] = (first_ref[...] * filtered).astype(jnp.bfloat16)


def short_part(features, halo, short_filter, decay_rate):
    _, tokens, channels = features.shape
    modes = decay_rate.shape[0]
    f32 = jnp.float32
    return pl.pallas_call(
        short_kernel,
        grid=(channels // LANES,),
        in_specs=[
            pl.BlockSpec((3, tokens, LANES), lambda c: (0, 0, c)),
            pl.BlockSpec((3, HALO, LANES), lambda c: (0, 0, c)),
            pl.BlockSpec((3, TAPS, LANES), lambda c: (0, 0, c)),
            pl.BlockSpec((modes, LANES), lambda c: (0, c)),
        ],
        out_specs=[
            pl.BlockSpec((tokens, LANES), lambda c: (0, c)),
            pl.BlockSpec((tokens, LANES), lambda c: (0, c)),
            pl.BlockSpec((SEGMENTS, modes, LANES), lambda c: (0, 0, c)),
            pl.BlockSpec((modes, LANES), lambda c: (0, c)),
        ],
        out_shape=[
            jax.ShapeDtypeStruct((tokens, channels), jnp.bfloat16),
            jax.ShapeDtypeStruct((tokens, channels), f32),
            jax.ShapeDtypeStruct((SEGMENTS, modes, channels), f32),
            jax.ShapeDtypeStruct((modes, channels), f32),
        ],
        scratch_shapes=[
            pltpu.VMEM((3, HALO + tokens, LANES), f32),
            pltpu.VMEM((tokens, LANES), f32),
            pltpu.VMEM((modes * SEGMENTS, LANES), f32),
        ],
        compiler_params=pltpu.CompilerParams(vmem_limit_bytes=24 * MIB),
        cost_estimate=pl.CostEstimate(flops=100 * tokens * channels, bytes_accessed=13 * tokens * channels, transcendentals=0),
        name="short_and_end_states",
    )(features, halo, short_filter, decay_rate)


def long_part(gated, first, enter, state, decay_rate, residue, skip_gain):
    tokens, channels = gated.shape
    modes = decay_rate.shape[0]
    f32 = jnp.float32
    by_token = pl.BlockSpec((tokens, LANES), lambda c: (0, c))
    by_mode = pl.BlockSpec((modes, LANES), lambda c: (0, c))
    return pl.pallas_call(
        long_kernel,
        grid=(channels // LANES,),
        in_specs=[
            by_token,
            by_token,
            pl.BlockSpec((SEGMENTS, modes, LANES), lambda c: (0, 0, c)),
            by_mode,
            by_mode,
            by_mode,
            pl.BlockSpec((1, LANES), lambda c: (0, c)),
        ],
        out_specs=by_token,
        out_shape=jax.ShapeDtypeStruct((tokens, channels), jnp.bfloat16),
        scratch_shapes=[
            pltpu.VMEM((tokens, LANES), f32),
            pltpu.VMEM((tokens, LANES), f32),
            pltpu.VMEM((SEGMENTS * modes, LANES), f32),
        ],
        compiler_params=pltpu.CompilerParams(vmem_limit_bytes=24 * MIB),
        cost_estimate=pl.CostEstimate(flops=100 * tokens * channels, bytes_accessed=10 * tokens * channels, transcendentals=0),
        name="modal_filter",
    )(gated, first, enter, state, decay_rate, residue, skip_gain[None])


def entering_states(ends, decay_rate, tokens):
    count = lax.axis_size("ctx")

    def power(k):
        return jnp.exp(-float(k * tokens) * decay_rate)

    near = shifted(ends, "ctx", 1)
    for j in range(2, min(RADIX, count - 1) + 1):
        near = near + power(j - 1) * shifted(ends, "ctx", j)
    state = near
    for m in range(RADIX, count, RADIX):
        state = state + power(m) * shifted(near, "ctx", m)
    return state


def normed_product(place_ref, *refs, pieces, steps):
    x_refs, (gain_ref, w_ref, out_ref, normed_ref, acc) = refs[:pieces], refs[pieces:]
    stream, k = pl.program_id(0), pl.program_id(1)
    per_piece = x_refs[0].shape[1]
    rows = w_ref.shape[0] * w_ref.shape[2]

    @pl.when((stream == 0) & (k == 0))
    def _():
        squares = 0.0
        for x_ref in x_refs:
            as_float = x_ref[...].astype(jnp.float32)
            squares = squares + jnp.sum(as_float * as_float, axis=1, keepdims=True)
        inverse = lax.rsqrt(squares / (pieces * per_piece) + EPSILON)
        for p, x_ref in enumerate(x_refs):
            at = lax.rem(place_ref[0] + p, pieces)
            gain = gain_ref[pl.ds(at, 1), :]
            scaled = (x_ref[...].astype(jnp.float32) * inverse * gain).astype(jnp.bfloat16)
            for part in range(per_piece // rows):
                normed_ref[p * (per_piece // rows) + part] = scaled[:, part * rows : (part + 1) * rows]

    weights = w_ref[:, 0].reshape(rows, w_ref.shape[3])
    term = jnp.dot(normed_ref[k], weights, preferred_element_type=jnp.float32)

    @pl.when(k == 0)
    def _():
        acc[...] = term

    @pl.when(k > 0)
    def _():
        acc[...] += term

    @pl.when(k == steps - 1)
    def _():
        out_ref[0] = acc[...].astype(jnp.bfloat16)


def product_only(place_ref, x_ref, w_ref, out_ref, acc, *, steps):
    k = pl.program_id(1)
    rows = w_ref.shape[0] * w_ref.shape[2]
    weights = w_ref[:, 0].reshape(rows, w_ref.shape[3])
    term = jnp.dot(x_ref[0], weights, preferred_element_type=jnp.float32)

    @pl.when(k == 0)
    def _():
        acc[...] = term

    @pl.when(k > 0)
    def _():
        acc[...] += term

    @pl.when(k == steps - 1)
    def _():
        out_ref[0] = acc[...].astype(jnp.bfloat16)


def weight_group(weights, pieces):
    shards, _, rows, _ = weights.shape
    return math.gcd(4, shards // pieces), rows


def project_first(place, xs, gain, weights):
    pieces = len(xs)
    tokens, per_piece = xs[0].shape
    shards, streams, rows, cols = weights.shape
    group, rows = weight_group(weights, pieces)
    steps = shards // group
    each = steps // pieces

    def weight_at(j, k, place):
        return (lax.rem(place[0] + k // each, pieces) * each + lax.rem(k, each), j, 0, 0)

    whole = pl.BlockSpec((tokens, per_piece), lambda j, k, place: (0, 0))
    return pl.pallas_call(
        functools.partial(normed_product, pieces=pieces, steps=steps),
        grid_spec=pltpu.PrefetchScalarGridSpec(
            num_scalar_prefetch=1,
            grid=(streams, steps),
            in_specs=[whole] * pieces
            + [
                pl.BlockSpec((pieces, per_piece), lambda j, k, place: (0, 0)),
                pl.BlockSpec((group, 1, rows, cols), weight_at),
            ],
            out_specs=[
                pl.BlockSpec((1, tokens, cols), lambda j, k, place: (j, 0, 0)),
                pl.BlockSpec((steps, tokens, group * rows), lambda j, k, place: (0, 0, 0)),
            ],
            scratch_shapes=[pltpu.VMEM((tokens, cols), jnp.float32)],
        ),
        out_shape=[
            jax.ShapeDtypeStruct((streams, tokens, cols), jnp.bfloat16),
            jax.ShapeDtypeStruct((steps, tokens, group * rows), jnp.bfloat16),
        ],
        compiler_params=pltpu.CompilerParams(vmem_limit_bytes=48 * MIB),
        cost_estimate=pl.CostEstimate(flops=2 * tokens * shards * rows * cols * streams, bytes_accessed=weights.size * 2, transcendentals=0),
        name="norm_keys_values",
    )(place, *xs, gain.reshape(pieces, per_piece), weights)


def project_rest(place, normed, weights, pieces):
    steps, tokens, _ = normed.shape
    shards, streams, rows, cols = weights.shape
    group, rows = weight_group(weights, pieces)
    each = steps // pieces

    def weight_at(j, k, place):
        return (lax.rem(place[0] + k // each, pieces) * each + lax.rem(k, each), j, 0, 0)

    return pl.pallas_call(
        functools.partial(product_only, steps=steps),
        grid_spec=pltpu.PrefetchScalarGridSpec(
            num_scalar_prefetch=1,
            grid=(streams, steps),
            in_specs=[
                pl.BlockSpec((1, tokens, group * rows), lambda j, k, place: (k, 0, 0)),
                pl.BlockSpec((group, 1, rows, cols), weight_at),
            ],
            out_specs=pl.BlockSpec((1, tokens, cols), lambda j, k, place: (j, 0, 0)),
            scratch_shapes=[pltpu.VMEM((tokens, cols), jnp.float32)],
        ),
        out_shape=jax.ShapeDtypeStruct((streams, tokens, cols), jnp.bfloat16),
        compiler_params=pltpu.CompilerParams(vmem_limit_bytes=32 * MIB),
        cost_estimate=pl.CostEstimate(flops=2 * tokens * shards * rows * cols * streams, bytes_accessed=weights.size * 2, transcendentals=0),
        name="project_queries",
    )(place, normed, weights)


def attend_kernel(position_ref, q_ref, *refs):
    kv_refs, out_ref = refs[:-1], refs[-1]
    tokens = q_ref.shape[1]
    tile = math.gcd(tokens, 256)
    contract = (((1,), (1,)), ((), ()))
    for r in range(tokens // tile):
        query = q_ref[0, r * tile : (r + 1) * tile]
        scores = []
        for lag, ref in enumerate(kv_refs):
            keys = (r + 1) * tile if lag == 0 else tokens
            s = lax.dot_general(query, ref[0, :keys], contract, preferred_element_type=jnp.float32) * (1.0 / math.sqrt(HD))
            if lag == 0:
                row = r * tile + lax.broadcasted_iota(jnp.int32, s.shape, 0)
                s = jnp.where(row >= lax.broadcasted_iota(jnp.int32, s.shape, 1), s, -jnp.inf)
            else:
                s = jnp.where(position_ref[0] >= lag, s, -jnp.inf)
            scores.append(s)
        peak = functools.reduce(jnp.maximum, [jnp.max(s, axis=1, keepdims=True) for s in scores])
        total, output = 0.0, 0.0
        for s, ref in zip(scores, kv_refs):
            expo = jnp.exp(s - peak)
            total = total + jnp.sum(expo, axis=1, keepdims=True)
            output = output + jnp.dot(expo.astype(jnp.bfloat16), ref[1, : s.shape[1]], preferred_element_type=jnp.float32)
        out_ref[r * tile : (r + 1) * tile] = (output / total).astype(jnp.bfloat16)


def attend(position, query, blocks):
    _, tokens, cols = query.shape
    pair = pl.BlockSpec((2, tokens, HD), lambda h, position: (0, 0, h))
    return pl.pallas_call(
        attend_kernel,
        grid_spec=pltpu.PrefetchScalarGridSpec(
            num_scalar_prefetch=1,
            grid=(cols // HD,),
            in_specs=[pl.BlockSpec((1, tokens, HD), lambda h, position: (0, 0, h))] + [pair] * len(blocks),
            out_specs=pl.BlockSpec((tokens, HD), lambda h, position: (0, h)),
        ),
        out_shape=jax.ShapeDtypeStruct((tokens, cols), jnp.bfloat16),
        compiler_params=pltpu.CompilerParams(vmem_limit_bytes=32 * MIB),
        cost_estimate=pl.CostEstimate(flops=4 * tokens * tokens * 3 * cols, bytes_accessed=16 * tokens * cols, transcendentals=0),
        name="windowed_attention",
    )(position, query, *blocks)


def on_device(features, short_filter, decay_rate, residue, skip_gain, norm_gain, qkv_weight):
    streams = features.transpose(1, 0, 2)
    weights = qkv_weight.transpose(1, 0, 2)
    tokens = streams.shape[1]
    pieces = lax.axis_size("tp")
    key_value_rows = lax.all_gather(weights[1:], "ctx")
    halo = shifted(streams[:, tokens - HALO :], "ctx", 1)
    query_shard, halo = lax.optimization_barrier((weights[:1], halo))
    query_rows = lax.all_gather(query_shard, "ctx")
    gated, first, enter, ends = short_part(streams, halo, short_filter, decay_rate)
    state = entering_states(ends, decay_rate, tokens)
    mixer = long_part(gated, first, enter, state, decay_rate, residue, skip_gain)
    parts = [mixer]
    for step in range(1, pieces):
        parts.append(lax.ppermute(mixer, "tp", [(s, (s - step) % pieces) for s in range(pieces)]))
    place = lax.axis_index("tp").astype(jnp.int32).reshape(1)
    key_value, normed = project_first(place, parts, norm_gain, key_value_rows)
    blocks = [key_value] + [shifted(key_value, "ctx", lag) for lag in range(1, WINDOW)]
    query = project_rest(place, normed, query_rows, pieces)
    position = lax.axis_index("ctx").astype(jnp.int32).reshape(1)
    return (mixer, attend(position, query, blocks))


def solution(mesh):
    placed = (
        P("ctx", None, "tp"),
        P(None, None, "tp"),
        P(None, "tp"),
        P(None, "tp"),
        P("tp"),
        P(),
        P("ctx", None, "tp"),
    )
    return jax.shard_map(
        on_device,
        mesh=mesh,
        in_specs=placed,
        out_specs=(P("ctx", "tp"), P("ctx", "tp")),
        check_vma=False,
    )
```

```python
import functools
import math

import jax
import jax.numpy as jnp
from jax import lax
from jax.experimental import pallas as pl
from jax.experimental.pallas import tpu as pltpu
from jax.sharding import PartitionSpec as P

HD = 128
TAPS = 7
WINDOW = 3
EPSILON = 1e-06
LANES = 128
SEGMENTS = 8
HALO = 16
RADIX = 4
HALVES = 2
MIB = 1 << 20


def shifted(value, axis, steps):
    count = lax.axis_size(axis)
    return lax.ppermute(value, axis, [(source, source + steps) for source in range(count - steps)])


def mode_rows(values, modes):
    return [jnp.broadcast_to(values[n : n + 1], (SEGMENTS, LANES)) for n in range(modes)]


def short_kernel(feat_ref, halo_ref, taps_ref, decay_ref, gated_ref, first_ref, enter_ref, end_ref, ext, gs, ends):
    tokens = feat_ref.shape[1]
    seg = tokens // SEGMENTS
    modes = decay_ref.shape[0]
    streams = []
    for j in range(3):
        ext[j, :HALO] = halo_ref[j].astype(jnp.float32)
        ext[j, HALO:] = feat_ref[j].astype(jnp.float32)
        total = taps_ref[j, 0:1] * ext[j, HALO:]
        for i in range(1, TAPS):
            total = total + taps_ref[j, i : i + 1] * ext[j, HALO - i : HALO - i + tokens]
        if j == 0:
            first_ref[...] = total
        elif j == 1:
            gs[...] = total
        else:
            gated = (gs[...] * total).astype(jnp.bfloat16)
    gated_ref[...] = gated
    gs[...] = gated.astype(jnp.float32)
    rate = decay_ref[...]
    decays = mode_rows(jnp.exp(-rate), modes)

    def step(t, states):
        g = gs[pl.ds(t, SEGMENTS, stride=seg), :]
        return tuple(a * s + g for a, s in zip(decays, states))

    zero = jnp.zeros((SEGMENTS, LANES), jnp.float32)
    states = lax.fori_loop(0, seg, step, (zero,) * modes, unroll=8)
    for n in range(modes):
        ends[n * SEGMENTS : (n + 1) * SEGMENTS] = states[n]
    across = jnp.exp(-float(seg) * rate)
    entering = jnp.zeros((modes, LANES), jnp.float32)
    for j in range(SEGMENTS):
        enter_ref[j] = entering
        entering = across * entering + ends[pl.ds(j, modes, stride=SEGMENTS), :]
    end_ref[...] = entering


def long_kernel(gated_ref, first_ref, enter_ref, state_ref, decay_ref, residue_ref, skip_ref, mixer_ref, gs, ys, starts):
    tokens = gated_ref.shape[0]
    seg = tokens // SEGMENTS
    modes = decay_ref.shape[0]
    rate = decay_ref[...]
    gs[...] = gated_ref[...].astype(jnp.float32)
    for j in range(SEGMENTS):
        starts[j * modes : (j + 1) * modes] = enter_ref[j] + jnp.exp(-float(j * seg) * rate) * state_ref[...]
    decays = mode_rows(jnp.exp(-rate), modes)
    weights = mode_rows(residue_ref[...] * jnp.sqrt(rate), modes)
    skip = jnp.broadcast_to(skip_ref[...], (SEGMENTS, LANES))

    def step(t, states):
        g = gs[pl.ds(t, SEGMENTS, stride=seg), :]
        states = tuple(a * s + g for a, s in zip(decays, states))
        terms = [w * s for w, s in zip(weights, states)]
        while len(terms) > 1:
            terms = [sum(terms[i : i + 2]) for i in range(0, len(terms), 2)]
        ys[pl.ds(t, SEGMENTS, stride=seg), :] = terms[0] + skip * g
        return states

    first = tuple(starts[pl.ds(n, SEGMENTS, stride=modes), :] for n in range(modes))
    lax.fori_loop(0, seg, step, first, unroll=8)
    filtered = ys[...].astype(jnp.bfloat16).astype(jnp.float32)
    mixer_ref[...] = (first_ref[...] * filtered).astype(jnp.bfloat16)


def short_part(features, halo, short_filter, decay_rate):
    _, tokens, channels = features.shape
    modes = decay_rate.shape[0]
    f32 = jnp.float32
    return pl.pallas_call(
        short_kernel,
        grid=(channels // LANES,),
        in_specs=[
            pl.BlockSpec((3, tokens, LANES), lambda c: (0, 0, c)),
            pl.BlockSpec((3, HALO, LANES), lambda c: (0, 0, c)),
            pl.BlockSpec((3, TAPS, LANES), lambda c: (0, 0, c)),
            pl.BlockSpec((modes, LANES), lambda c: (0, c)),
        ],
        out_specs=[
            pl.BlockSpec((tokens, LANES), lambda c: (0, c)),
            pl.BlockSpec((tokens, LANES), lambda c: (0, c)),
            pl.BlockSpec((SEGMENTS, modes, LANES), lambda c: (0, 0, c)),
            pl.BlockSpec((modes, LANES), lambda c: (0, c)),
        ],
        out_shape=[
            jax.ShapeDtypeStruct((tokens, channels), jnp.bfloat16),
            jax.ShapeDtypeStruct((tokens, channels), f32),
            jax.ShapeDtypeStruct((SEGMENTS, modes, channels), f32),
            jax.ShapeDtypeStruct((modes, channels), f32),
        ],
        scratch_shapes=[
            pltpu.VMEM((3, HALO + tokens, LANES), f32),
            pltpu.VMEM((tokens, LANES), f32),
            pltpu.VMEM((modes * SEGMENTS, LANES), f32),
        ],
        compiler_params=pltpu.CompilerParams(vmem_limit_bytes=24 * MIB),
        cost_estimate=pl.CostEstimate(flops=100 * tokens * channels, bytes_accessed=13 * tokens * channels, transcendentals=0),
        name="short_and_end_states",
    )(features, halo, short_filter, decay_rate)


def long_part(gated, first, enter, state, decay_rate, residue, skip_gain, half):
    tokens, channels = gated.shape
    channels = channels // HALVES
    ahead = half * (channels // LANES)
    modes = decay_rate.shape[0]
    f32 = jnp.float32
    by_token = pl.BlockSpec((tokens, LANES), lambda c: (0, c + ahead))
    by_mode = pl.BlockSpec((modes, LANES), lambda c: (0, c + ahead))
    return pl.pallas_call(
        long_kernel,
        grid=(channels // LANES,),
        in_specs=[
            by_token,
            by_token,
            pl.BlockSpec((SEGMENTS, modes, LANES), lambda c: (0, 0, c + ahead)),
            by_mode,
            by_mode,
            by_mode,
            pl.BlockSpec((1, LANES), lambda c: (0, c + ahead)),
        ],
        out_specs=pl.BlockSpec((tokens, LANES), lambda c: (0, c)),
        out_shape=jax.ShapeDtypeStruct((tokens, channels), jnp.bfloat16),
        scratch_shapes=[
            pltpu.VMEM((tokens, LANES), f32),
            pltpu.VMEM((tokens, LANES), f32),
            pltpu.VMEM((SEGMENTS * modes, LANES), f32),
        ],
        compiler_params=pltpu.CompilerParams(vmem_limit_bytes=24 * MIB),
        cost_estimate=pl.CostEstimate(flops=100 * tokens * channels, bytes_accessed=10 * tokens * channels, transcendentals=0),
        name="modal_filter",
    )(gated, first, enter, state, decay_rate, residue, skip_gain[None])


def entering_states(ends, decay_rate, tokens):
    count = lax.axis_size("ctx")

    def power(k):
        return jnp.exp(-float(k * tokens) * decay_rate)

    near = shifted(ends, "ctx", 1)
    for j in range(2, min(RADIX, count - 1) + 1):
        near = near + power(j - 1) * shifted(ends, "ctx", j)
    state = near
    for m in range(RADIX, count, RADIX):
        state = state + power(m) * shifted(near, "ctx", m)
    return state


def norm_kernel(place_ref, *refs, pieces):
    x_refs, (gain_ref, out_ref) = refs[:-2], refs[-2:]
    split = len(x_refs) // pieces
    width = x_refs[0].shape[1]
    rows = out_ref.shape[2]
    squares = 0.0
    for x_ref in x_refs:
        as_float = x_ref[...].astype(jnp.float32)
        squares = squares + jnp.sum(as_float * as_float, axis=1, keepdims=True)
    inverse = lax.rsqrt(squares / (len(x_refs) * width) + EPSILON)
    each = width // rows
    for p, x_ref in enumerate(x_refs):
        at = lax.rem(place_ref[0] + p // split, pieces) * split + p % split
        gain = gain_ref[pl.ds(at, 1), :]
        scaled = (x_ref[...].astype(jnp.float32) * inverse * gain).astype(jnp.bfloat16)
        for part in range(each):
            out_ref[p * each + part] = scaled[:, part * rows : (part + 1) * rows]


def norm_part(place, xs, gain, pieces, rows):
    tokens, width = xs[0].shape
    tile = math.gcd(tokens, 128)
    steps = len(xs) * width // rows
    return pl.pallas_call(
        functools.partial(norm_kernel, pieces=pieces),
        grid_spec=pltpu.PrefetchScalarGridSpec(
            num_scalar_prefetch=1,
            grid=(tokens // tile,),
            in_specs=[pl.BlockSpec((tile, width), lambda t, place: (t, 0))] * len(xs)
            + [pl.BlockSpec((len(xs), width), lambda t, place: (0, 0))],
            out_specs=pl.BlockSpec((steps, tile, rows), lambda t, place: (0, t, 0)),
        ),
        out_shape=jax.ShapeDtypeStruct((steps, tokens, rows), jnp.bfloat16),
        compiler_params=pltpu.CompilerParams(vmem_limit_bytes=32 * MIB),
        cost_estimate=pl.CostEstimate(flops=8 * tokens * width * len(xs), bytes_accessed=4 * tokens * width * len(xs), transcendentals=0),
        name="norm",
    )(place, *xs, gain.reshape(len(xs), width))


def product_kernel(place_ref, x_ref, *refs, steps):
    w_refs, (out_ref, acc) = refs[:-2], refs[-2:]
    k = pl.program_id(0)
    for i, w_ref in enumerate(w_refs):
        weights = w_ref[:, 0].reshape(w_ref.shape[0] * w_ref.shape[2], w_ref.shape[3])
        term = jnp.dot(x_ref[0], weights, preferred_element_type=jnp.float32)

        @pl.when(k == 0)
        def _():
            acc[i] = term

        @pl.when((k > 0) & (k < steps - 1))
        def _():
            acc[i] += term

        @pl.when(k == steps - 1)
        def _():
            out_ref[i] = (acc[i] + term).astype(jnp.bfloat16)


def project(place, normed, weights, pieces, group, streams, half, halves):
    steps, tokens, depth = normed.shape
    _, _, rows, cols = weights.shape
    cols = cols // halves
    each = steps // pieces

    def weight_at(stream):
        return lambda k, place: (lax.rem(place[0] + k // each, pieces) * each + lax.rem(k, each), stream, 0, half)

    return pl.pallas_call(
        functools.partial(product_kernel, steps=steps),
        grid_spec=pltpu.PrefetchScalarGridSpec(
            num_scalar_prefetch=1,
            grid=(steps,),
            in_specs=[pl.BlockSpec((1, tokens, depth), lambda k, place: (k, 0, 0))]
            + [pl.BlockSpec((group, 1, rows, cols), weight_at(stream)) for stream in streams],
            out_specs=pl.BlockSpec((len(streams), tokens, cols), lambda k, place: (0, 0, 0)),
            scratch_shapes=[pltpu.VMEM((len(streams), tokens, cols), jnp.float32)],
        ),
        out_shape=jax.ShapeDtypeStruct((len(streams), tokens, cols), jnp.bfloat16),
        compiler_params=pltpu.CompilerParams(vmem_limit_bytes=32 * MIB),
        cost_estimate=pl.CostEstimate(
            flops=2 * steps * tokens * depth * cols * len(streams),
            bytes_accessed=2 * steps * depth * (tokens + cols * len(streams)),
            transcendentals=0,
        ),
        name="project",
    )(place, normed, *[weights] * len(streams))


def attend_kernel(position_ref, q_ref, *refs):
    own_ref, near_ref, even_ref, odd_ref = refs[:4]
    out_ref, far = refs[-2:]
    even = lax.rem(position_ref[0], 2) == 0

    @pl.when(even)
    def _():
        far[...] = even_ref[...]

    @pl.when(jnp.logical_not(even))
    def _():
        far[...] = odd_ref[...]

    kv_refs = (own_ref, near_ref, far)
    tokens = q_ref.shape[1]
    tile = math.gcd(tokens, 256)
    contract = (((1,), (1,)), ((), ()))
    for r in range(tokens // tile):
        query = q_ref[0, r * tile : (r + 1) * tile]
        scores = []
        for lag, ref in enumerate(kv_refs):
            keys = (r + 1) * tile if lag == 0 else tokens
            s = lax.dot_general(query, ref[0, :keys], contract, preferred_element_type=jnp.float32) * (1.0 / math.sqrt(HD))
            if lag == 0:
                row = r * tile + lax.broadcasted_iota(jnp.int32, s.shape, 0)
                s = jnp.where(row >= lax.broadcasted_iota(jnp.int32, s.shape, 1), s, -jnp.inf)
            else:
                s = jnp.where(position_ref[0] >= lag, s, -jnp.inf)
            scores.append(s)
        peak = functools.reduce(jnp.maximum, [jnp.max(s, axis=1, keepdims=True) for s in scores])
        total, output = 0.0, 0.0
        for s, ref in zip(scores, kv_refs):
            expo = jnp.exp(s - peak)
            total = total + jnp.sum(expo, axis=1, keepdims=True)
            output = output + jnp.dot(expo.astype(jnp.bfloat16), ref[1, : s.shape[1]], preferred_element_type=jnp.float32)
        out_ref[r * tile : (r + 1) * tile] = (output / total).astype(jnp.bfloat16)


def attend(position, query, blocks, half, before):
    _, tokens, cols = query.shape
    heads = cols // HD // HALVES
    ahead = half * heads
    pair = pl.BlockSpec((2, tokens, HD), lambda h, position: (0, 0, h))
    extra = [] if before is None else [before]
    return pl.pallas_call(
        attend_kernel,
        grid_spec=pltpu.PrefetchScalarGridSpec(
            num_scalar_prefetch=1,
            grid=(heads,),
            in_specs=[pl.BlockSpec((1, tokens, HD), lambda h, position: (0, 0, h + ahead))]
            + [pair] * len(blocks)
            + [pl.BlockSpec(memory_space=pl.ANY)] * len(extra),
            out_specs=pl.BlockSpec((tokens, HD), lambda h, position: (0, h + ahead)),
            scratch_shapes=[pltpu.VMEM((2, tokens, HD), jnp.bfloat16)],
        ),
        out_shape=jax.ShapeDtypeStruct((tokens, cols), jnp.bfloat16),
        input_output_aliases={2 + len(blocks): 0} if extra else {},
        compiler_params=pltpu.CompilerParams(vmem_limit_bytes=32 * MIB),
        cost_estimate=pl.CostEstimate(flops=4 * tokens * tokens * 3 * cols // HALVES, bytes_accessed=16 * tokens * cols // HALVES, transcendentals=0),
        name="windowed_attention",
    )(position, query, *blocks, *extra)


def window_blocks(own):
    count = lax.axis_size("ctx")
    near = shifted(own, "ctx", 1)
    even = lax.ppermute(own, "ctx", [(s, s + 2) for s in range(0, count - 2, 2)])
    odd = lax.ppermute(near, "ctx", [(s, s + 1) for s in range(0, count - 1, 2)])
    return (own, near, even, odd)


def on_device(features, short_filter, decay_rate, residue, skip_gain, norm_gain, qkv_weight):
    streams = features.transpose(1, 0, 2)
    weights = qkv_weight.transpose(1, 0, 2)
    tokens = streams.shape[1]
    pieces = lax.axis_size("tp")
    rows = lax.all_gather(weights, "ctx")
    halo = shifted(streams[:, tokens - HALO :], "ctx", 1)
    gated, first, enter, ends = short_part(streams, halo, short_filter, decay_rate)
    state = entering_states(ends, decay_rate, tokens)
    own = []
    others = [[] for _ in range(1, pieces)]
    for half in range(HALVES):
        own.append(long_part(gated, first, enter, state, decay_rate, residue, skip_gain, half))
        for step in range(1, pieces):
            source = [(s, (s - step) % pieces) for s in range(pieces)]
            others[step - 1].append(lax.ppermute(own[-1], "tp", source))
    parts = own + [part for group in others for part in group]
    place = lax.axis_index("tp").astype(jnp.int32).reshape(1)
    group = math.gcd(4, rows.shape[0] // len(parts))
    normed = norm_part(place, parts, norm_gain, pieces, group * rows.shape[2])
    windows = []
    for half in range(HALVES):
        pair = project(place, normed, rows, pieces, group, (1, 2), half, HALVES)
        windows.append(window_blocks(pair))
    query = project(place, normed, rows, pieces, group, (0,), 0, 1)
    position = lax.axis_index("ctx").astype(jnp.int32).reshape(1)
    attended = None
    for half in range(HALVES):
        attended = attend(position, query, windows[half], half, attended)
    return (jnp.concatenate(own, axis=1), attended)


def solution(mesh):
    placed = (
        P("ctx", None, "tp"),
        P(None, None, "tp"),
        P(None, "tp"),
        P(None, "tp"),
        P("tp"),
        P(),
        P("ctx", None, "tp"),
    )
    return jax.shard_map(
        on_device,
        mesh=mesh,
        in_specs=placed,
        out_specs=(P("ctx", "tp"), P("ctx", "tp")),
        check_vma=False,
    )
```

```python
import functools
import math

import jax
import jax.numpy as jnp
from jax import lax
from jax.experimental import pallas as pl
from jax.experimental.pallas import tpu as pltpu
from jax.sharding import PartitionSpec as P

HD = 128
TAPS = 7
WINDOW = 3
EPSILON = 1e-06
LANES = 128
SEGMENTS = 8
HALO = 16
RADIX = 4
HALVES = 2
MIB = 1 << 20


def shifted(value, axis, steps):
    count = lax.axis_size(axis)
    return lax.ppermute(value, axis, [(source, source + steps) for source in range(count - steps)])


def mode_rows(values, modes):
    return [jnp.broadcast_to(values[n : n + 1], (SEGMENTS, LANES)) for n in range(modes)]


def short_kernel(feat_ref, halo_ref, taps_ref, decay_ref, gated_ref, first_ref, enter_ref, end_ref, ext, gs, ends):
    tokens = feat_ref.shape[1]
    seg = tokens // SEGMENTS
    modes = decay_ref.shape[0]
    streams = []
    for j in range(3):
        ext[j, :HALO] = halo_ref[j].astype(jnp.float32)
        ext[j, HALO:] = feat_ref[j].astype(jnp.float32)
        total = taps_ref[j, 0:1] * ext[j, HALO:]
        for i in range(1, TAPS):
            total = total + taps_ref[j, i : i + 1] * ext[j, HALO - i : HALO - i + tokens]
        if j == 0:
            first_ref[...] = total
        elif j == 1:
            gs[...] = total
        else:
            gated = (gs[...] * total).astype(jnp.bfloat16)
    gated_ref[...] = gated
    gs[...] = gated.astype(jnp.float32)
    rate = decay_ref[...]
    decays = mode_rows(jnp.exp(-rate), modes)

    def step(t, states):
        g = gs[pl.ds(t, SEGMENTS, stride=seg), :]
        return tuple(a * s + g for a, s in zip(decays, states))

    zero = jnp.zeros((SEGMENTS, LANES), jnp.float32)
    states = lax.fori_loop(0, seg, step, (zero,) * modes, unroll=8)
    for n in range(modes):
        ends[n * SEGMENTS : (n + 1) * SEGMENTS] = states[n]
    across = jnp.exp(-float(seg) * rate)
    entering = jnp.zeros((modes, LANES), jnp.float32)
    for j in range(SEGMENTS):
        enter_ref[j] = entering
        entering = across * entering + ends[pl.ds(j, modes, stride=SEGMENTS), :]
    end_ref[...] = entering


def long_kernel(gated_ref, first_ref, enter_ref, state_ref, decay_ref, residue_ref, skip_ref, mixer_ref, gs, ys, starts):
    tokens = gated_ref.shape[0]
    seg = tokens // SEGMENTS
    modes = decay_ref.shape[0]
    rate = decay_ref[...]
    gs[...] = gated_ref[...].astype(jnp.float32)
    for j in range(SEGMENTS):
        starts[j * modes : (j + 1) * modes] = enter_ref[j] + jnp.exp(-float(j * seg) * rate) * state_ref[...]
    decays = mode_rows(jnp.exp(-rate), modes)
    weights = mode_rows(residue_ref[...] * jnp.sqrt(rate), modes)
    skip = jnp.broadcast_to(skip_ref[...], (SEGMENTS, LANES))

    def step(t, states):
        g = gs[pl.ds(t, SEGMENTS, stride=seg), :]
        states = tuple(a * s + g for a, s in zip(decays, states))
        terms = [w * s for w, s in zip(weights, states)]
        while len(terms) > 1:
            terms = [sum(terms[i : i + 2]) for i in range(0, len(terms), 2)]
        ys[pl.ds(t, SEGMENTS, stride=seg), :] = terms[0] + skip * g
        return states

    first = tuple(starts[pl.ds(n, SEGMENTS, stride=modes), :] for n in range(modes))
    lax.fori_loop(0, seg, step, first, unroll=8)
    filtered = ys[...].astype(jnp.bfloat16).astype(jnp.float32)
    mixer_ref[...] = (first_ref[...] * filtered).astype(jnp.bfloat16)


def short_part(features, halo, short_filter, decay_rate):
    _, tokens, channels = features.shape
    modes = decay_rate.shape[0]
    f32 = jnp.float32
    return pl.pallas_call(
        short_kernel,
        grid=(channels // LANES,),
        in_specs=[
            pl.BlockSpec((3, tokens, LANES), lambda c: (0, 0, c)),
            pl.BlockSpec((3, HALO, LANES), lambda c: (0, 0, c)),
            pl.BlockSpec((3, TAPS, LANES), lambda c: (0, 0, c)),
            pl.BlockSpec((modes, LANES), lambda c: (0, c)),
        ],
        out_specs=[
            pl.BlockSpec((tokens, LANES), lambda c: (0, c)),
            pl.BlockSpec((tokens, LANES), lambda c: (0, c)),
            pl.BlockSpec((SEGMENTS, modes, LANES), lambda c: (0, 0, c)),
            pl.BlockSpec((modes, LANES), lambda c: (0, c)),
        ],
        out_shape=[
            jax.ShapeDtypeStruct((tokens, channels), jnp.bfloat16),
            jax.ShapeDtypeStruct((tokens, channels), f32),
            jax.ShapeDtypeStruct((SEGMENTS, modes, channels), f32),
            jax.ShapeDtypeStruct((modes, channels), f32),
        ],
        scratch_shapes=[
            pltpu.VMEM((3, HALO + tokens, LANES), f32),
            pltpu.VMEM((tokens, LANES), f32),
            pltpu.VMEM((modes * SEGMENTS, LANES), f32),
        ],
        compiler_params=pltpu.CompilerParams(vmem_limit_bytes=24 * MIB),
        cost_estimate=pl.CostEstimate(flops=100 * tokens * channels, bytes_accessed=13 * tokens * channels, transcendentals=0),
        name="short_and_end_states",
    )(features, halo, short_filter, decay_rate)


def long_part(gated, first, enter, state, decay_rate, residue, skip_gain, half):
    tokens, channels = gated.shape
    channels = channels // HALVES
    ahead = half * (channels // LANES)
    modes = decay_rate.shape[0]
    f32 = jnp.float32
    by_token = pl.BlockSpec((tokens, LANES), lambda c: (0, c + ahead))
    by_mode = pl.BlockSpec((modes, LANES), lambda c: (0, c + ahead))
    return pl.pallas_call(
        long_kernel,
        grid=(channels // LANES,),
        in_specs=[
            by_token,
            by_token,
            pl.BlockSpec((SEGMENTS, modes, LANES), lambda c: (0, 0, c + ahead)),
            by_mode,
            by_mode,
            by_mode,
            pl.BlockSpec((1, LANES), lambda c: (0, c + ahead)),
        ],
        out_specs=pl.BlockSpec((tokens, LANES), lambda c: (0, c)),
        out_shape=jax.ShapeDtypeStruct((tokens, channels), jnp.bfloat16),
        scratch_shapes=[
            pltpu.VMEM((tokens, LANES), f32),
            pltpu.VMEM((tokens, LANES), f32),
            pltpu.VMEM((SEGMENTS * modes, LANES), f32),
        ],
        compiler_params=pltpu.CompilerParams(vmem_limit_bytes=24 * MIB),
        cost_estimate=pl.CostEstimate(flops=100 * tokens * channels, bytes_accessed=10 * tokens * channels, transcendentals=0),
        name="modal_filter",
    )(gated, first, enter, state, decay_rate, residue, skip_gain[None])


def entering_states(ends, decay_rate, tokens):
    count = lax.axis_size("ctx")

    def power(k):
        return jnp.exp(-float(k * tokens) * decay_rate)

    def from_before(value, steps):
        return shifted(value, "ctx", steps).astype(jnp.float32)

    sent = ends.astype(jnp.bfloat16)
    near = from_before(sent, 1)
    for j in range(2, min(RADIX, count - 1) + 1):
        near = near + power(j - 1) * from_before(sent, j)
    state = near
    sent = near.astype(jnp.bfloat16)
    for m in range(RADIX, count, RADIX):
        state = state + power(m) * from_before(sent, m)
    return state


def norm_kernel(place_ref, *refs, pieces):
    x_refs, (gain_ref, out_ref) = refs[:-2], refs[-2:]
    split = len(x_refs) // pieces
    width = x_refs[0].shape[1]
    rows = out_ref.shape[2]
    squares = 0.0
    for x_ref in x_refs:
        as_float = x_ref[...].astype(jnp.float32)
        squares = squares + jnp.sum(as_float * as_float, axis=1, keepdims=True)
    inverse = lax.rsqrt(squares / (len(x_refs) * width) + EPSILON)
    each = width // rows
    for p, x_ref in enumerate(x_refs):
        at = lax.rem(place_ref[0] + p // split, pieces) * split + p % split
        gain = gain_ref[pl.ds(at, 1), :]
        scaled = (x_ref[...].astype(jnp.float32) * inverse * gain).astype(jnp.bfloat16)
        for part in range(each):
            out_ref[at * each + part] = scaled[:, part * rows : (part + 1) * rows]


def norm_part(place, xs, gain, pieces, rows):
    tokens, width = xs[0].shape
    tile = math.gcd(tokens, 128)
    steps = len(xs) * width // rows
    return pl.pallas_call(
        functools.partial(norm_kernel, pieces=pieces),
        grid_spec=pltpu.PrefetchScalarGridSpec(
            num_scalar_prefetch=1,
            grid=(tokens // tile,),
            in_specs=[pl.BlockSpec((tile, width), lambda t, place: (t, 0))] * len(xs)
            + [pl.BlockSpec((len(xs), width), lambda t, place: (0, 0))],
            out_specs=pl.BlockSpec((steps, tile, rows), lambda t, place: (0, t, 0)),
        ),
        out_shape=jax.ShapeDtypeStruct((steps, tokens, rows), jnp.bfloat16),
        compiler_params=pltpu.CompilerParams(vmem_limit_bytes=32 * MIB),
        cost_estimate=pl.CostEstimate(flops=8 * tokens * width * len(xs), bytes_accessed=4 * tokens * width * len(xs), transcendentals=0),
        name="norm",
    )(place, *xs, gain.reshape(len(xs), width))


def head_attention(query, pairs, position, tokens):
    tile = math.gcd(tokens, 256)
    contract = (((1,), (1,)), ((), ()))
    outputs = []
    for r in range(tokens // tile):
        rows = query[r * tile : (r + 1) * tile]
        scores = []
        for lag, (keys, _) in enumerate(pairs):
            if lag == 0:
                keys = keys[: (r + 1) * tile]
            s = lax.dot_general(rows, keys, contract, preferred_element_type=jnp.float32) * (1.0 / math.sqrt(HD))
            if lag == 0:
                row = r * tile + lax.broadcasted_iota(jnp.int32, s.shape, 0)
                s = jnp.where(row >= lax.broadcasted_iota(jnp.int32, s.shape, 1), s, -jnp.inf)
            else:
                s = jnp.where(position >= lag, s, -jnp.inf)
            scores.append(s)
        peak = functools.reduce(jnp.maximum, [jnp.max(s, axis=1, keepdims=True) for s in scores])
        total, output = 0.0, 0.0
        for s, (_, values) in zip(scores, pairs):
            expo = jnp.exp(s - peak)
            total = total + jnp.sum(expo, axis=1, keepdims=True)
            output = output + jnp.dot(expo.astype(jnp.bfloat16), values[: s.shape[1]], preferred_element_type=jnp.float32)
        outputs.append((output / total).astype(jnp.bfloat16))
    return outputs


def attention_kernel(
    normed_ref, rows_ref, out_ref, w_kv, w_q, own, near, far, query, load_sem, near_send, near_recv, far_send, far_recv, relay_send
):
    count = lax.axis_size("ctx")
    me = lax.axis_index("ctx")
    even = lax.rem(me, 2) == 0
    chunks, _, tokens, width = own.shape
    steps, _, depth = normed_ref.shape
    group = rows_ref.shape[0] // steps
    has_next, has_before = me < count - 1, me >= 1
    sends_far = even & (me < count - 2)
    gets_far = me >= 2
    relays = even & (me >= 2)

    def load(c, stream):
        source = rows_ref.at[:, stream, :, c * width : (c + 1) * width]
        target = w_q.at[c] if stream == 0 else w_kv.at[c, stream - 1]
        return pltpu.make_async_copy(source, target, load_sem.at[c, stream])

    def wait_load(c, stream):
        target = w_q.at[c] if stream == 0 else w_kv.at[c, stream - 1]
        pltpu.make_async_copy(target, target, load_sem.at[c, stream]).wait()

    def remote(source, target, send, recv, device):
        return pltpu.make_async_remote_copy(
            src_ref=source,
            dst_ref=target,
            send_sem=send,
            recv_sem=recv,
            device_id={"ctx": device},
            device_id_type=pl.DeviceIdType.MESH,
        )

    def send_near(c):
        return remote(own.at[c], near.at[c], near_send.at[c], near_recv.at[c], me + 1)

    def send_far(c):
        return remote(own.at[c], far.at[c], far_send.at[c], far_recv.at[c], me + 2)

    def send_relay(c):
        return remote(near.at[c], far.at[c], relay_send.at[c], far_recv.at[c], me + 1)

    for c in range(chunks):
        for stream in (1, 2):
            load(c, stream).start()
    for c in range(chunks):
        load(c, 0).start()

    barrier = pltpu.get_barrier_semaphore()
    for there, step in ((has_next, 1), (has_before, -1), (sends_far, 2), (relays, -2)):

        @pl.when(there)
        def _():
            pl.semaphore_signal(barrier, inc=1, device_id={"ctx": me + step}, device_id_type=pl.DeviceIdType.MESH)

    greeted = [jnp.where(there, 1, 0) for there in (has_next, has_before, sends_far, relays)]
    pl.semaphore_wait(barrier, sum(greeted))

    @pl.when(jnp.logical_not(has_before))
    def _():
        near[...] = jnp.zeros_like(near)

    @pl.when(jnp.logical_not(gets_far))
    def _():
        far[...] = jnp.zeros_like(far)

    def product(weights):
        total = 0.0
        for k in range(steps):
            part = weights[k * group : (k + 1) * group].reshape(depth, width)
            total = total + jnp.dot(normed_ref[k], part, preferred_element_type=jnp.float32)
        return total.astype(jnp.bfloat16)

    @pl.loop(0, chunks)
    def _(c):
        for i in range(2):
            wait_load(c, i + 1)
            own[c, i] = product(w_kv.at[c, i])

        @pl.when(has_next)
        def _():
            send_near(c).start()

        @pl.when(sends_far)
        def _():
            send_far(c).start()

    @pl.loop(0, chunks)
    def _(c):
        wait_load(c, 0)
        query[c] = product(w_q.at[c])

    @pl.loop(0, chunks)
    def _(c):
        @pl.when(has_before)
        def _():
            send_near(c).wait_recv()

        @pl.when(relays)
        def _():
            send_relay(c).start()

        @pl.when(gets_far)
        def _():
            send_far(c).wait_recv()

        for head in range(width // HD):
            cols = slice(head * HD, (head + 1) * HD)
            pairs = [(ref[c, 0, :, cols], ref[c, 1, :, cols]) for ref in (own, near, far)]
            outputs = head_attention(query[c, :, cols], pairs, me, tokens)
            tile = tokens // len(outputs)
            for r, value in enumerate(outputs):
                out_ref[c, r * tile : (r + 1) * tile, cols] = value

    @pl.loop(0, chunks)
    def _(c):
        @pl.when(has_next)
        def _():
            send_near(c).wait_send()

        @pl.when(sends_far)
        def _():
            send_far(c).wait_send()

        @pl.when(relays)
        def _():
            send_relay(c).wait_send()


def attention_part(normed, rows):
    steps, tokens, depth = normed.shape
    shards, _, per_shard, cols = rows.shape
    width = min(cols, 2 * HD)
    chunks = cols // width
    bf16 = jnp.bfloat16
    out = pl.pallas_call(
        attention_kernel,
        in_specs=[pl.BlockSpec(memory_space=pltpu.VMEM), pl.BlockSpec(memory_space=pl.ANY)],
        out_specs=pl.BlockSpec(memory_space=pltpu.VMEM),
        out_shape=jax.ShapeDtypeStruct((chunks, tokens, width), bf16),
        scratch_shapes=[
            pltpu.VMEM((chunks, 2, shards, per_shard, width), bf16),
            pltpu.VMEM((chunks, shards, per_shard, width), bf16),
            pltpu.VMEM((chunks, 2, tokens, width), bf16),
            pltpu.VMEM((chunks, 2, tokens, width), bf16),
            pltpu.VMEM((chunks, 2, tokens, width), bf16),
            pltpu.VMEM((chunks, tokens, width), bf16),
            pltpu.SemaphoreType.DMA((chunks, 3)),
        ]
        + [pltpu.SemaphoreType.DMA((chunks,))] * 5,
        compiler_params=pltpu.CompilerParams(vmem_limit_bytes=52 * MIB, collective_id=0, has_side_effects=True),
        cost_estimate=pl.CostEstimate(
            flops=2 * tokens * shards * per_shard * cols * 3, bytes_accessed=rows.size * 2, transcendentals=0
        ),
        name="projections_and_attention",
    )(normed, rows)
    return out.transpose(1, 0, 2).reshape(tokens, cols)


def on_device(features, short_filter, decay_rate, residue, skip_gain, norm_gain, qkv_weight):
    streams = features.transpose(1, 0, 2)
    weights = qkv_weight.transpose(1, 0, 2)
    tokens = streams.shape[1]
    pieces = lax.axis_size("tp")
    rows = lax.all_gather(weights, "ctx")
    halo = shifted(streams[:, tokens - HALO :], "ctx", 1)
    gated, first, enter, ends = short_part(streams, halo, short_filter, decay_rate)
    state = entering_states(ends, decay_rate, tokens)
    own = []
    others = [[] for _ in range(1, pieces)]
    for half in range(HALVES):
        own.append(long_part(gated, first, enter, state, decay_rate, residue, skip_gain, half))
        for step in range(1, pieces):
            source = [(s, (s - step) % pieces) for s in range(pieces)]
            others[step - 1].append(lax.ppermute(own[-1], "tp", source))
    parts = own + [part for group in others for part in group]
    place = lax.axis_index("tp").astype(jnp.int32).reshape(1)
    group = math.gcd(4, rows.shape[0] // len(parts))
    normed = norm_part(place, parts, norm_gain, pieces, group * rows.shape[2])
    return (jnp.concatenate(own, axis=1), attention_part(normed, rows))


def solution(mesh):
    placed = (
        P("ctx", None, "tp"),
        P(None, None, "tp"),
        P(None, "tp"),
        P(None, "tp"),
        P("tp"),
        P(),
        P("ctx", None, "tp"),
    )
    return jax.shard_map(
        on_device,
        mesh=mesh,
        in_specs=placed,
        out_specs=(P("ctx", "tp"), P("ctx", "tp")),
        check_vma=False,
    )
```

```python
import functools
import math

import jax
import jax.numpy as jnp
from jax import lax
from jax.experimental import pallas as pl
from jax.experimental.pallas import tpu as pltpu
from jax.sharding import PartitionSpec as P

HD = 128
TAPS = 7
WINDOW = 3
EPSILON = 1e-06
LANES = 128
SEGMENTS = 8
HALO = 16
RADIX = 4
HALVES = 2
MIB = 1 << 20


def shifted(value, axis, steps):
    count = lax.axis_size(axis)
    return lax.ppermute(value, axis, [(source, source + steps) for source in range(count - steps)])


def mode_rows(values, modes):
    return [jnp.broadcast_to(values[n : n + 1], (SEGMENTS, LANES)) for n in range(modes)]


def short_kernel(feat_ref, halo_ref, taps_ref, decay_ref, gated_ref, first_ref, enter_ref, end_ref, ext, gs, ends):
    tokens = feat_ref.shape[1]
    seg = tokens // SEGMENTS
    modes = decay_ref.shape[0]
    streams = []
    for j in range(3):
        ext[j, :HALO] = halo_ref[j].astype(jnp.float32)
        ext[j, HALO:] = feat_ref[j].astype(jnp.float32)
        total = taps_ref[j, 0:1] * ext[j, HALO:]
        for i in range(1, TAPS):
            total = total + taps_ref[j, i : i + 1] * ext[j, HALO - i : HALO - i + tokens]
        if j == 0:
            first_ref[...] = total
        elif j == 1:
            gs[...] = total
        else:
            gated = (gs[...] * total).astype(jnp.bfloat16)
    gated_ref[...] = gated
    gs[...] = gated.astype(jnp.float32)
    rate = decay_ref[...]
    decays = mode_rows(jnp.exp(-rate), modes)

    def step(t, states):
        g = gs[pl.ds(t, SEGMENTS, stride=seg), :]
        return tuple(a * s + g for a, s in zip(decays, states))

    zero = jnp.zeros((SEGMENTS, LANES), jnp.float32)
    states = lax.fori_loop(0, seg, step, (zero,) * modes, unroll=8)
    for n in range(modes):
        ends[n * SEGMENTS : (n + 1) * SEGMENTS] = states[n]
    across = jnp.exp(-float(seg) * rate)
    entering = jnp.zeros((modes, LANES), jnp.float32)
    for j in range(SEGMENTS):
        enter_ref[j] = entering
        entering = across * entering + ends[pl.ds(j, modes, stride=SEGMENTS), :]
    end_ref[...] = entering


def long_kernel(gated_ref, first_ref, enter_ref, state_ref, decay_ref, residue_ref, skip_ref, mixer_ref, gs, ys, starts):
    tokens = gated_ref.shape[0]
    seg = tokens // SEGMENTS
    modes = decay_ref.shape[0]
    rate = decay_ref[...]
    gs[...] = gated_ref[...].astype(jnp.float32)
    for j in range(SEGMENTS):
        starts[j * modes : (j + 1) * modes] = enter_ref[j] + jnp.exp(-float(j * seg) * rate) * state_ref[...]
    decays = mode_rows(jnp.exp(-rate), modes)
    weights = mode_rows(residue_ref[...] * jnp.sqrt(rate), modes)
    skip = jnp.broadcast_to(skip_ref[...], (SEGMENTS, LANES))

    def step(t, states):
        g = gs[pl.ds(t, SEGMENTS, stride=seg), :]
        states = tuple(a * s + g for a, s in zip(decays, states))
        terms = [w * s for w, s in zip(weights, states)]
        while len(terms) > 1:
            terms = [sum(terms[i : i + 2]) for i in range(0, len(terms), 2)]
        ys[pl.ds(t, SEGMENTS, stride=seg), :] = terms[0] + skip * g
        return states

    first = tuple(starts[pl.ds(n, SEGMENTS, stride=modes), :] for n in range(modes))
    lax.fori_loop(0, seg, step, first, unroll=8)
    filtered = ys[...].astype(jnp.bfloat16).astype(jnp.float32)
    mixer_ref[...] = (first_ref[...] * filtered).astype(jnp.bfloat16)


def short_part(features, halo, short_filter, decay_rate):
    _, tokens, channels = features.shape
    modes = decay_rate.shape[0]
    f32 = jnp.float32
    return pl.pallas_call(
        short_kernel,
        grid=(channels // LANES,),
        in_specs=[
            pl.BlockSpec((3, tokens, LANES), lambda c: (0, 0, c)),
            pl.BlockSpec((3, HALO, LANES), lambda c: (0, 0, c)),
            pl.BlockSpec((3, TAPS, LANES), lambda c: (0, 0, c)),
            pl.BlockSpec((modes, LANES), lambda c: (0, c)),
        ],
        out_specs=[
            pl.BlockSpec((tokens, LANES), lambda c: (0, c)),
            pl.BlockSpec((tokens, LANES), lambda c: (0, c)),
            pl.BlockSpec((SEGMENTS, modes, LANES), lambda c: (0, 0, c)),
            pl.BlockSpec((modes, LANES), lambda c: (0, c)),
        ],
        out_shape=[
            jax.ShapeDtypeStruct((tokens, channels), jnp.bfloat16),
            jax.ShapeDtypeStruct((tokens, channels), f32),
            jax.ShapeDtypeStruct((SEGMENTS, modes, channels), f32),
            jax.ShapeDtypeStruct((modes, channels), f32),
        ],
        scratch_shapes=[
            pltpu.VMEM((3, HALO + tokens, LANES), f32),
            pltpu.VMEM((tokens, LANES), f32),
            pltpu.VMEM((modes * SEGMENTS, LANES), f32),
        ],
        compiler_params=pltpu.CompilerParams(vmem_limit_bytes=24 * MIB),
        cost_estimate=pl.CostEstimate(flops=100 * tokens * channels, bytes_accessed=13 * tokens * channels, transcendentals=0),
        name="short_and_end_states",
    )(features, halo, short_filter, decay_rate)


def long_part(gated, first, enter, state, decay_rate, residue, skip_gain, half):
    tokens, channels = gated.shape
    channels = channels // HALVES
    ahead = half * (channels // LANES)
    modes = decay_rate.shape[0]
    f32 = jnp.float32
    by_token = pl.BlockSpec((tokens, LANES), lambda c: (0, c + ahead))
    by_mode = pl.BlockSpec((modes, LANES), lambda c: (0, c + ahead))
    return pl.pallas_call(
        long_kernel,
        grid=(channels // LANES,),
        in_specs=[
            by_token,
            by_token,
            pl.BlockSpec((SEGMENTS, modes, LANES), lambda c: (0, 0, c + ahead)),
            by_mode,
            by_mode,
            by_mode,
            pl.BlockSpec((1, LANES), lambda c: (0, c + ahead)),
        ],
        out_specs=pl.BlockSpec((tokens, LANES), lambda c: (0, c)),
        out_shape=jax.ShapeDtypeStruct((tokens, channels), jnp.bfloat16),
        scratch_shapes=[
            pltpu.VMEM((tokens, LANES), f32),
            pltpu.VMEM((tokens, LANES), f32),
            pltpu.VMEM((SEGMENTS * modes, LANES), f32),
        ],
        compiler_params=pltpu.CompilerParams(vmem_limit_bytes=24 * MIB),
        cost_estimate=pl.CostEstimate(flops=100 * tokens * channels, bytes_accessed=10 * tokens * channels, transcendentals=0),
        name="modal_filter",
    )(gated, first, enter, state, decay_rate, residue, skip_gain[None])


def entering_states(ends, decay_rate, tokens):
    count = lax.axis_size("ctx")

    def power(k):
        return jnp.exp(-float(k * tokens) * decay_rate)

    def from_before(value, steps):
        return shifted(value, "ctx", steps).astype(jnp.float32)

    sent = ends.astype(jnp.bfloat16)
    near = from_before(sent, 1)
    for j in range(2, min(RADIX, count - 1) + 1):
        near = near + power(j - 1) * from_before(sent, j)
    state = near
    sent = near.astype(jnp.bfloat16)
    for m in range(RADIX, count, RADIX):
        state = state + power(m) * from_before(sent, m)
    return state


def norm_kernel(place_ref, *refs, pieces):
    x_refs, (gain_ref, out_ref) = refs[:-2], refs[-2:]
    split = len(x_refs) // pieces
    width = x_refs[0].shape[1]
    rows = out_ref.shape[2]
    squares = 0.0
    for x_ref in x_refs:
        as_float = x_ref[...].astype(jnp.float32)
        squares = squares + jnp.sum(as_float * as_float, axis=1, keepdims=True)
    inverse = lax.rsqrt(squares / (len(x_refs) * width) + EPSILON)
    each = width // rows
    for p, x_ref in enumerate(x_refs):
        at = lax.rem(place_ref[0] + p // split, pieces) * split + p % split
        gain = gain_ref[pl.ds(at, 1), :]
        scaled = (x_ref[...].astype(jnp.float32) * inverse * gain).astype(jnp.bfloat16)
        for part in range(each):
            out_ref[at * each + part] = scaled[:, part * rows : (part + 1) * rows]


def norm_part(place, xs, gain, pieces, rows):
    tokens, width = xs[0].shape
    tile = math.gcd(tokens, 128)
    steps = len(xs) * width // rows
    return pl.pallas_call(
        functools.partial(norm_kernel, pieces=pieces),
        grid_spec=pltpu.PrefetchScalarGridSpec(
            num_scalar_prefetch=1,
            grid=(tokens // tile,),
            in_specs=[pl.BlockSpec((tile, width), lambda t, place: (t, 0))] * len(xs)
            + [pl.BlockSpec((len(xs), width), lambda t, place: (0, 0))],
            out_specs=pl.BlockSpec((steps, tile, rows), lambda t, place: (0, t, 0)),
        ),
        out_shape=jax.ShapeDtypeStruct((steps, tokens, rows), jnp.bfloat16),
        compiler_params=pltpu.CompilerParams(vmem_limit_bytes=32 * MIB),
        cost_estimate=pl.CostEstimate(flops=8 * tokens * width * len(xs), bytes_accessed=4 * tokens * width * len(xs), transcendentals=0),
        name="norm",
    )(place, *xs, gain.reshape(len(xs), width))


def partial_attention(query, first_row, blocks, position):
    contract = (((1,), (1,)), ((), ()))
    scores = []
    for lag, keys, _ in blocks:
        s = lax.dot_general(query, keys, contract, preferred_element_type=jnp.float32) * (1.0 / math.sqrt(HD))
        if lag == 0:
            row = first_row + lax.broadcasted_iota(jnp.int32, s.shape, 0)
            s = jnp.where(row >= lax.broadcasted_iota(jnp.int32, s.shape, 1), s, -jnp.inf)
        else:
            s = jnp.where(position >= lag, s, -jnp.inf)
        scores.append(s)
    peak = functools.reduce(jnp.maximum, [jnp.max(s, axis=1, keepdims=True) for s in scores])
    return scores, peak


def weigh(scores, peak, blocks):
    total, output = 0.0, 0.0
    for s, (_, _, values) in zip(scores, blocks):
        expo = jnp.exp(s - peak)
        total = total + jnp.sum(expo, axis=1, keepdims=True)
        output = output + jnp.dot(expo.astype(jnp.bfloat16), values, preferred_element_type=jnp.float32)
    return total, output


def attention_kernel(
    normed_ref, rows_ref, out_ref, w_kv, w_q, own, near, far, query, load_sem, near_send, near_recv, far_send, far_recv, relay_send, peaks, totals, outputs
):
    count = lax.axis_size("ctx")
    me = lax.axis_index("ctx")
    even = lax.rem(me, 2) == 0
    chunks, _, tokens, width = own.shape
    steps, _, depth = normed_ref.shape
    group = rows_ref.shape[0] // steps
    has_next, has_before = me < count - 1, me >= 1
    sends_far = even & (me < count - 2)
    gets_far = me >= 2
    relays = even & (me >= 2)

    def load(c, stream):
        source = rows_ref.at[:, stream, :, pl.ds(pl.multiple_of(c * width, width), width)]
        target = w_q.at[c] if stream == 0 else w_kv.at[c, stream - 1]
        return pltpu.make_async_copy(source, target, load_sem.at[c, stream])

    def wait_load(c, stream):
        target = w_q.at[c] if stream == 0 else w_kv.at[c, stream - 1]
        pltpu.make_async_copy(target, target, load_sem.at[c, stream]).wait()

    def remote(source, target, send, recv, device):
        return pltpu.make_async_remote_copy(
            src_ref=source,
            dst_ref=target,
            send_sem=send,
            recv_sem=recv,
            device_id={"ctx": device},
            device_id_type=pl.DeviceIdType.MESH,
        )

    def send_near(c):
        return remote(own.at[c], near.at[c], near_send.at[c], near_recv.at[c], me + 1)

    def send_far(c):
        return remote(own.at[c], far.at[c], far_send.at[c], far_recv.at[c], me + 2)

    def send_relay(c):
        return remote(near.at[c], far.at[c], relay_send.at[c], far_recv.at[c], me + 1)

    for stream in (1, 2):
        load(0, stream).start()

    barrier = pltpu.get_barrier_semaphore()
    for there, step in ((has_next, 1), (has_before, -1), (sends_far, 2), (relays, -2)):

        @pl.when(there)
        def _():
            pl.semaphore_signal(barrier, inc=1, device_id={"ctx": me + step}, device_id_type=pl.DeviceIdType.MESH)

    greeted = [jnp.where(there, 1, 0) for there in (has_next, has_before, sends_far, relays)]
    pl.semaphore_wait(barrier, sum(greeted))

    @pl.when(jnp.logical_not(has_before))
    def _():
        near[...] = jnp.zeros_like(near)

    @pl.when(jnp.logical_not(gets_far))
    def _():
        far[...] = jnp.zeros_like(far)

    def product(weights):
        total = 0.0
        for k in range(steps):
            part = weights[k * group : (k + 1) * group].reshape(depth, width)
            total = total + jnp.dot(normed_ref[k], part, preferred_element_type=jnp.float32)
        return total.astype(jnp.bfloat16)

    @pl.loop(0, chunks)
    def _(c):
        @pl.when(c < chunks - 1)
        def _():
            for stream in (1, 2):
                load(c + 1, stream).start()

        load(c, 0).start()
        for i in range(2):
            wait_load(c, i + 1)
            own[c, i] = product(w_kv.at[c, i])

        @pl.when(has_next)
        def _():
            send_near(c).start()

        @pl.when(sends_far)
        def _():
            send_far(c).start()

    @pl.loop(0, chunks)
    def _(c):
        wait_load(c, 0)
        query[c] = product(w_q.at[c])

    @pl.loop(0, chunks)
    def _(c):
        @pl.when(has_before)
        def _():
            send_near(c).wait_recv()

        @pl.when(relays)
        def _():
            send_relay(c).start()

        tile = math.gcd(tokens, 256)
        tiles = [(head * HD, r * tile) for head in range(width // HD) for r in range(tokens // tile)]

        def block(ref, lag, col, keys):
            return lag, ref[c, 0, :keys, col : col + HD], ref[c, 1, :keys, col : col + HD]

        for at, (col, row) in enumerate(tiles):
            blocks = [block(own, 0, col, row + tile), block(near, 1, col, tokens)]
            scores, peak = partial_attention(query[c, row : row + tile, col : col + HD], row, blocks, me)
            total, output = weigh(scores, peak, blocks)
            peaks[at], totals[at], outputs[at] = peak, total, output

        @pl.when(gets_far)
        def _():
            send_far(c).wait_recv()

        for at, (col, row) in enumerate(tiles):
            blocks = [block(far, 2, col, tokens)]
            scores, peak = partial_attention(query[c, row : row + tile, col : col + HD], row, blocks, me)
            both = jnp.maximum(peak, peaks[at])
            total, output = weigh(scores, both, blocks)
            scale = jnp.exp(peaks[at] - both)
            output = (outputs[at] * scale + output) / (totals[at] * scale + total)
            out_ref[c, row : row + tile, col : col + HD] = output.astype(jnp.bfloat16)

    @pl.loop(0, chunks)
    def _(c):
        @pl.when(has_next)
        def _():
            send_near(c).wait_send()

        @pl.when(sends_far)
        def _():
            send_far(c).wait_send()

        @pl.when(relays)
        def _():
            send_relay(c).wait_send()


def attention_part(normed, rows):
    steps, tokens, depth = normed.shape
    shards, _, per_shard, cols = rows.shape
    width = min(cols, 2 * HD)
    chunks = cols // width
    tile = math.gcd(tokens, 256)
    tiles = (width // HD) * (tokens // tile)
    bf16 = jnp.bfloat16
    out = pl.pallas_call(
        attention_kernel,
        in_specs=[pl.BlockSpec(memory_space=pltpu.VMEM), pl.BlockSpec(memory_space=pl.ANY)],
        out_specs=pl.BlockSpec(memory_space=pltpu.VMEM),
        out_shape=jax.ShapeDtypeStruct((chunks, tokens, width), bf16),
        scratch_shapes=[
            pltpu.VMEM((chunks, 2, shards, per_shard, width), bf16),
            pltpu.VMEM((chunks, shards, per_shard, width), bf16),
            pltpu.VMEM((chunks, 2, tokens, width), bf16),
            pltpu.VMEM((chunks, 2, tokens, width), bf16),
            pltpu.VMEM((chunks, 2, tokens, width), bf16),
            pltpu.VMEM((chunks, tokens, width), bf16),
            pltpu.SemaphoreType.DMA((chunks, 3)),
        ]
        + [pltpu.SemaphoreType.DMA((chunks,))] * 5
        + [pltpu.VMEM((tiles, tile, 1), jnp.float32)] * 2
        + [pltpu.VMEM((tiles, tile, HD), jnp.float32)],
        compiler_params=pltpu.CompilerParams(vmem_limit_bytes=52 * MIB, collective_id=0, has_side_effects=True),
        cost_estimate=pl.CostEstimate(
            flops=2 * tokens * shards * per_shard * cols * 3, bytes_accessed=rows.size * 2, transcendentals=0
        ),
        name="projections_and_attention",
    )(normed, rows)
    return out.transpose(1, 0, 2).reshape(tokens, cols)


def on_device(features, short_filter, decay_rate, residue, skip_gain, norm_gain, qkv_weight):
    streams = features.transpose(1, 0, 2)
    weights = qkv_weight.transpose(1, 0, 2)
    tokens = streams.shape[1]
    pieces = lax.axis_size("tp")
    rows = lax.all_gather(weights, "ctx")
    halo = shifted(streams[:, tokens - HALO :], "ctx", 1)
    gated, first, enter, ends = short_part(streams, halo, short_filter, decay_rate)
    state = entering_states(ends, decay_rate, tokens)
    own = []
    others = [[] for _ in range(1, pieces)]
    for half in range(HALVES):
        own.append(long_part(gated, first, enter, state, decay_rate, residue, skip_gain, half))
        for step in range(1, pieces):
            source = [(s, (s - step) % pieces) for s in range(pieces)]
            others[step - 1].append(lax.ppermute(own[-1], "tp", source))
    parts = own + [part for group in others for part in group]
    place = lax.axis_index("tp").astype(jnp.int32).reshape(1)
    group = math.gcd(4, rows.shape[0] // len(parts))
    normed = norm_part(place, parts, norm_gain, pieces, group * rows.shape[2])
    return (jnp.concatenate(own, axis=1), attention_part(normed, rows))


def solution(mesh):
    placed = (
        P("ctx", None, "tp"),
        P(None, None, "tp"),
        P(None, "tp"),
        P(None, "tp"),
        P("tp"),
        P(),
        P("ctx", None, "tp"),
    )
    return jax.shard_map(
        on_device,
        mesh=mesh,
        in_specs=placed,
        out_specs=(P("ctx", "tp"), P("ctx", "tp")),
        check_vma=False,
    )
```

```python
import functools
import math

import jax
import jax.numpy as jnp
from jax import lax
from jax.experimental import pallas as pl
from jax.experimental.pallas import tpu as pltpu
from jax.sharding import PartitionSpec as P

HD = 128
TAPS = 7
WINDOW = 3
EPSILON = 1e-06
LANES = 128
SEGMENTS = 8
HALO = 16
RADIX = 4
HALVES = 2
MIB = 1 << 20


def shifted(value, axis, steps):
    count = lax.axis_size(axis)
    return lax.ppermute(value, axis, [(source, source + steps) for source in range(count - steps)])


def mode_rows(values, modes):
    return [jnp.broadcast_to(values[n : n + 1], (SEGMENTS, LANES)) for n in range(modes)]


def short_kernel(feat_ref, halo_ref, taps_ref, decay_ref, gated_ref, first_ref, enter_ref, end_ref, ext, gs, ends):
    tokens = feat_ref.shape[1]
    seg = tokens // SEGMENTS
    modes = decay_ref.shape[0]
    streams = []
    for j in range(3):
        ext[j, :HALO] = halo_ref[j].astype(jnp.float32)
        ext[j, HALO:] = feat_ref[j].astype(jnp.float32)
        total = taps_ref[j, 0:1] * ext[j, HALO:]
        for i in range(1, TAPS):
            total = total + taps_ref[j, i : i + 1] * ext[j, HALO - i : HALO - i + tokens]
        if j == 0:
            first_ref[...] = total
        elif j == 1:
            gs[...] = total
        else:
            gated = (gs[...] * total).astype(jnp.bfloat16)
    gated_ref[...] = gated
    gs[...] = gated.astype(jnp.float32)
    rate = decay_ref[...]
    decays = mode_rows(jnp.exp(-rate), modes)

    def step(t, states):
        g = gs[pl.ds(t, SEGMENTS, stride=seg), :]
        return tuple(a * s + g for a, s in zip(decays, states))

    zero = jnp.zeros((SEGMENTS, LANES), jnp.float32)
    states = lax.fori_loop(0, seg, step, (zero,) * modes, unroll=8)
    for n in range(modes):
        ends[n * SEGMENTS : (n + 1) * SEGMENTS] = states[n]
    across = jnp.exp(-float(seg) * rate)
    entering = jnp.zeros((modes, LANES), jnp.float32)
    for j in range(SEGMENTS):
        enter_ref[j] = entering
        entering = across * entering + ends[pl.ds(j, modes, stride=SEGMENTS), :]
    end_ref[...] = entering


def long_kernel(gated_ref, first_ref, enter_ref, state_ref, decay_ref, residue_ref, skip_ref, mixer_ref, gs, ys, starts):
    tokens = gated_ref.shape[0]
    seg = tokens // SEGMENTS
    modes = decay_ref.shape[0]
    rate = decay_ref[...]
    gs[...] = gated_ref[...].astype(jnp.float32)
    for j in range(SEGMENTS):
        starts[j * modes : (j + 1) * modes] = enter_ref[j] + jnp.exp(-float(j * seg) * rate) * state_ref[...]
    decays = mode_rows(jnp.exp(-rate), modes)
    weights = mode_rows(residue_ref[...] * jnp.sqrt(rate), modes)
    skip = jnp.broadcast_to(skip_ref[...], (SEGMENTS, LANES))

    def step(t, states):
        g = gs[pl.ds(t, SEGMENTS, stride=seg), :]
        states = tuple(a * s + g for a, s in zip(decays, states))
        terms = [w * s for w, s in zip(weights, states)]
        while len(terms) > 1:
            terms = [sum(terms[i : i + 2]) for i in range(0, len(terms), 2)]
        ys[pl.ds(t, SEGMENTS, stride=seg), :] = terms[0] + skip * g
        return states

    first = tuple(starts[pl.ds(n, SEGMENTS, stride=modes), :] for n in range(modes))
    lax.fori_loop(0, seg, step, first, unroll=8)
    filtered = ys[...].astype(jnp.bfloat16).astype(jnp.float32)
    mixer_ref[...] = (first_ref[...] * filtered).astype(jnp.bfloat16)


def short_part(features, halo, short_filter, decay_rate):
    _, tokens, channels = features.shape
    modes = decay_rate.shape[0]
    f32 = jnp.float32
    return pl.pallas_call(
        short_kernel,
        grid=(channels // LANES,),
        in_specs=[
            pl.BlockSpec((3, tokens, LANES), lambda c: (0, 0, c)),
            pl.BlockSpec((3, HALO, LANES), lambda c: (0, 0, c)),
            pl.BlockSpec((3, TAPS, LANES), lambda c: (0, 0, c)),
            pl.BlockSpec((modes, LANES), lambda c: (0, c)),
        ],
        out_specs=[
            pl.BlockSpec((tokens, LANES), lambda c: (0, c)),
            pl.BlockSpec((tokens, LANES), lambda c: (0, c)),
            pl.BlockSpec((SEGMENTS, modes, LANES), lambda c: (0, 0, c)),
            pl.BlockSpec((modes, LANES), lambda c: (0, c)),
        ],
        out_shape=[
            jax.ShapeDtypeStruct((tokens, channels), jnp.bfloat16),
            jax.ShapeDtypeStruct((tokens, channels), f32),
            jax.ShapeDtypeStruct((SEGMENTS, modes, channels), f32),
            jax.ShapeDtypeStruct((modes, channels), f32),
        ],
        scratch_shapes=[
            pltpu.VMEM((3, HALO + tokens, LANES), f32),
            pltpu.VMEM((tokens, LANES), f32),
            pltpu.VMEM((modes * SEGMENTS, LANES), f32),
        ],
        compiler_params=pltpu.CompilerParams(vmem_limit_bytes=24 * MIB),
        cost_estimate=pl.CostEstimate(flops=100 * tokens * channels, bytes_accessed=13 * tokens * channels, transcendentals=0),
        name="short_and_end_states",
    )(features, halo, short_filter, decay_rate)


def long_part(gated, first, enter, state, decay_rate, residue, skip_gain, half):
    tokens, channels = gated.shape
    channels = channels // HALVES
    ahead = half * (channels // LANES)
    modes = decay_rate.shape[0]
    f32 = jnp.float32
    by_token = pl.BlockSpec((tokens, LANES), lambda c: (0, c + ahead))
    by_mode = pl.BlockSpec((modes, LANES), lambda c: (0, c + ahead))
    return pl.pallas_call(
        long_kernel,
        grid=(channels // LANES,),
        in_specs=[
            by_token,
            by_token,
            pl.BlockSpec((SEGMENTS, modes, LANES), lambda c: (0, 0, c + ahead)),
            by_mode,
            by_mode,
            by_mode,
            pl.BlockSpec((1, LANES), lambda c: (0, c + ahead)),
        ],
        out_specs=pl.BlockSpec((tokens, LANES), lambda c: (0, c)),
        out_shape=jax.ShapeDtypeStruct((tokens, channels), jnp.bfloat16),
        scratch_shapes=[
            pltpu.VMEM((tokens, LANES), f32),
            pltpu.VMEM((tokens, LANES), f32),
            pltpu.VMEM((SEGMENTS * modes, LANES), f32),
        ],
        compiler_params=pltpu.CompilerParams(vmem_limit_bytes=24 * MIB),
        cost_estimate=pl.CostEstimate(flops=100 * tokens * channels, bytes_accessed=10 * tokens * channels, transcendentals=0),
        name="modal_filter",
    )(gated, first, enter, state, decay_rate, residue, skip_gain[None])


def entering_states(ends, decay_rate, tokens):
    count = lax.axis_size("ctx")

    def power(k):
        return jnp.exp(-float(k * tokens) * decay_rate)

    state = shifted(ends, "ctx", 1)
    step = 1
    while step < count:
        sent = state if step < RADIX else state.astype(jnp.bfloat16)
        state = state + power(step) * shifted(sent, "ctx", step).astype(jnp.float32)
        step *= 2
    return state


def norm_kernel(place_ref, *refs, pieces):
    x_refs, (gain_ref, out_ref) = refs[:-2], refs[-2:]
    split = len(x_refs) // pieces
    width = x_refs[0].shape[1]
    rows = out_ref.shape[2]
    squares = 0.0
    for x_ref in x_refs:
        as_float = x_ref[...].astype(jnp.float32)
        squares = squares + jnp.sum(as_float * as_float, axis=1, keepdims=True)
    inverse = lax.rsqrt(squares / (len(x_refs) * width) + EPSILON)
    each = width // rows
    for p, x_ref in enumerate(x_refs):
        at = lax.rem(place_ref[0] + p // split, pieces) * split + p % split
        gain = gain_ref[pl.ds(at, 1), :]
        scaled = (x_ref[...].astype(jnp.float32) * inverse * gain).astype(jnp.bfloat16)
        for part in range(each):
            out_ref[at * each + part] = scaled[:, part * rows : (part + 1) * rows]


def norm_part(place, xs, gain, pieces, rows):
    tokens, width = xs[0].shape
    tile = math.gcd(tokens, 128)
    steps = len(xs) * width // rows
    return pl.pallas_call(
        functools.partial(norm_kernel, pieces=pieces),
        grid_spec=pltpu.PrefetchScalarGridSpec(
            num_scalar_prefetch=1,
            grid=(tokens // tile,),
            in_specs=[pl.BlockSpec((tile, width), lambda t, place: (t, 0))] * len(xs)
            + [pl.BlockSpec((len(xs), width), lambda t, place: (0, 0))],
            out_specs=pl.BlockSpec((steps, tile, rows), lambda t, place: (0, t, 0)),
        ),
        out_shape=jax.ShapeDtypeStruct((steps, tokens, rows), jnp.bfloat16),
        compiler_params=pltpu.CompilerParams(vmem_limit_bytes=32 * MIB),
        cost_estimate=pl.CostEstimate(flops=8 * tokens * width * len(xs), bytes_accessed=4 * tokens * width * len(xs), transcendentals=0),
        name="norm",
    )(place, *xs, gain.reshape(len(xs), width))


def partial_attention(query, first_row, blocks, position):
    contract = (((1,), (1,)), ((), ()))
    scores = []
    for lag, keys, _ in blocks:
        s = lax.dot_general(query, keys, contract, preferred_element_type=jnp.float32) * (1.0 / math.sqrt(HD))
        if lag == 0:
            row = first_row + lax.broadcasted_iota(jnp.int32, s.shape, 0)
            s = jnp.where(row >= lax.broadcasted_iota(jnp.int32, s.shape, 1), s, -jnp.inf)
        else:
            s = jnp.where(position >= lag, s, -jnp.inf)
        scores.append(s)
    peak = functools.reduce(jnp.maximum, [jnp.max(s, axis=1, keepdims=True) for s in scores])
    return scores, peak


def weigh(scores, peak, blocks):
    total, output = 0.0, 0.0
    for s, (_, _, values) in zip(scores, blocks):
        expo = jnp.exp(s - peak)
        total = total + jnp.sum(expo, axis=1, keepdims=True)
        output = output + jnp.dot(expo.astype(jnp.bfloat16), values, preferred_element_type=jnp.float32)
    return total, output


def attention_kernel(
    normed_ref, rows_ref, out_ref, w_kv, w_q, own, near, far, query, load_sem, near_send, near_recv, far_send, far_recv, relay_send, peaks, totals, outputs
):
    count = lax.axis_size("ctx")
    me = lax.axis_index("ctx")
    even = lax.rem(me, 2) == 0
    chunks, _, tokens, width = own.shape
    steps, _, depth = normed_ref.shape
    group = rows_ref.shape[0] // steps
    has_next, has_before = me < count - 1, me >= 1
    sends_far = even & (me < count - 2)
    gets_far = me >= 2
    relays = even & (me >= 2)

    def load(c, stream):
        source = rows_ref.at[:, stream, :, pl.ds(pl.multiple_of(c * width, width), width)]
        target = w_q.at[c] if stream == 0 else w_kv.at[c, stream - 1]
        return pltpu.make_async_copy(source, target, load_sem.at[c, stream])

    def wait_load(c, stream):
        target = w_q.at[c] if stream == 0 else w_kv.at[c, stream - 1]
        pltpu.make_async_copy(target, target, load_sem.at[c, stream]).wait()

    def remote(source, target, send, recv, device):
        return pltpu.make_async_remote_copy(
            src_ref=source,
            dst_ref=target,
            send_sem=send,
            recv_sem=recv,
            device_id={"ctx": device},
            device_id_type=pl.DeviceIdType.MESH,
        )

    def send_near(c):
        return remote(own.at[c], near.at[c], near_send.at[c], near_recv.at[c], me + 1)

    def send_far(c):
        return remote(own.at[c], far.at[c], far_send.at[c], far_recv.at[c], me + 2)

    def send_relay(c):
        return remote(near.at[c], far.at[c], relay_send.at[c], far_recv.at[c], me + 1)

    for stream in (1, 2):
        load(0, stream).start()

    barrier = pltpu.get_barrier_semaphore()
    for there, step in ((has_next, 1), (has_before, -1), (sends_far, 2), (relays, -2)):

        @pl.when(there)
        def _():
            pl.semaphore_signal(barrier, inc=1, device_id={"ctx": me + step}, device_id_type=pl.DeviceIdType.MESH)

    greeted = [jnp.where(there, 1, 0) for there in (has_next, has_before, sends_far, relays)]
    pl.semaphore_wait(barrier, sum(greeted))

    @pl.when(jnp.logical_not(has_before))
    def _():
        near[...] = jnp.zeros_like(near)

    @pl.when(jnp.logical_not(gets_far))
    def _():
        far[...] = jnp.zeros_like(far)

    def product(weights):
        total = 0.0
        for k in range(steps):
            part = weights[k * group : (k + 1) * group].reshape(depth, width)
            total = total + jnp.dot(normed_ref[k], part, preferred_element_type=jnp.float32)
        return total.astype(jnp.bfloat16)

    @pl.loop(0, chunks)
    def _(c):
        @pl.when(c < chunks - 1)
        def _():
            for stream in (1, 2):
                load(c + 1, stream).start()

        load(c, 0).start()
        for i in range(2):
            wait_load(c, i + 1)
            own[c, i] = product(w_kv.at[c, i])

        @pl.when(has_next)
        def _():
            send_near(c).start()

        @pl.when(sends_far)
        def _():
            send_far(c).start()

    @pl.loop(0, chunks)
    def _(c):
        wait_load(c, 0)
        query[c] = product(w_q.at[c])

    @pl.loop(0, chunks)
    def _(c):
        @pl.when(has_before)
        def _():
            send_near(c).wait_recv()

        @pl.when(relays)
        def _():
            send_relay(c).start()

        tile = math.gcd(tokens, 256)
        tiles = [(head * HD, r * tile) for head in range(width // HD) for r in range(tokens // tile)]

        def block(ref, lag, col, keys):
            return lag, ref[c, 0, :keys, col : col + HD], ref[c, 1, :keys, col : col + HD]

        for at, (col, row) in enumerate(tiles):
            blocks = [block(own, 0, col, row + tile), block(near, 1, col, tokens)]
            scores, peak = partial_attention(query[c, row : row + tile, col : col + HD], row, blocks, me)
            total, output = weigh(scores, peak, blocks)
            peaks[at], totals[at], outputs[at] = peak, total, output

        @pl.when(gets_far)
        def _():
            send_far(c).wait_recv()

        for at, (col, row) in enumerate(tiles):
            blocks = [block(far, 2, col, tokens)]
            scores, peak = partial_attention(query[c, row : row + tile, col : col + HD], row, blocks, me)
            both = jnp.maximum(peak, peaks[at])
            total, output = weigh(scores, both, blocks)
            scale = jnp.exp(peaks[at] - both)
            output = (outputs[at] * scale + output) / (totals[at] * scale + total)
            out_ref[c, row : row + tile, col : col + HD] = output.astype(jnp.bfloat16)

    @pl.loop(0, chunks)
    def _(c):
        @pl.when(has_next)
        def _():
            send_near(c).wait_send()

        @pl.when(sends_far)
        def _():
            send_far(c).wait_send()

        @pl.when(relays)
        def _():
            send_relay(c).wait_send()


def attention_part(normed, rows):
    steps, tokens, depth = normed.shape
    shards, _, per_shard, cols = rows.shape
    width = min(cols, 2 * HD)
    chunks = cols // width
    tile = math.gcd(tokens, 256)
    tiles = (width // HD) * (tokens // tile)
    bf16 = jnp.bfloat16
    out = pl.pallas_call(
        attention_kernel,
        in_specs=[pl.BlockSpec(memory_space=pltpu.VMEM), pl.BlockSpec(memory_space=pl.ANY)],
        out_specs=pl.BlockSpec(memory_space=pltpu.VMEM),
        out_shape=jax.ShapeDtypeStruct((chunks, tokens, width), bf16),
        scratch_shapes=[
            pltpu.VMEM((chunks, 2, shards, per_shard, width), bf16),
            pltpu.VMEM((chunks, shards, per_shard, width), bf16),
            pltpu.VMEM((chunks, 2, tokens, width), bf16),
            pltpu.VMEM((chunks, 2, tokens, width), bf16),
            pltpu.VMEM((chunks, 2, tokens, width), bf16),
            pltpu.VMEM((chunks, tokens, width), bf16),
            pltpu.SemaphoreType.DMA((chunks, 3)),
        ]
        + [pltpu.SemaphoreType.DMA((chunks,))] * 5
        + [pltpu.VMEM((tiles, tile, 1), jnp.float32)] * 2
        + [pltpu.VMEM((tiles, tile, HD), jnp.float32)],
        compiler_params=pltpu.CompilerParams(vmem_limit_bytes=52 * MIB, collective_id=0, has_side_effects=True),
        cost_estimate=pl.CostEstimate(
            flops=2 * tokens * shards * per_shard * cols * 3, bytes_accessed=rows.size * 2, transcendentals=0
        ),
        name="projections_and_attention",
    )(normed, rows)
    return out.transpose(1, 0, 2).reshape(tokens, cols)


def on_device(features, short_filter, decay_rate, residue, skip_gain, norm_gain, qkv_weight):
    streams = features.transpose(1, 0, 2)
    weights = qkv_weight.transpose(1, 0, 2)
    tokens = streams.shape[1]
    pieces = lax.axis_size("tp")
    rows = lax.all_gather(weights, "ctx")
    halo = shifted(streams[:, tokens - HALO :], "ctx", 1)
    gated, first, enter, ends = short_part(streams, halo, short_filter, decay_rate)
    state = entering_states(ends, decay_rate, tokens)
    own = []
    others = [[] for _ in range(1, pieces)]
    for half in range(HALVES):
        own.append(long_part(gated, first, enter, state, decay_rate, residue, skip_gain, half))
        for step in range(1, pieces):
            source = [(s, (s - step) % pieces) for s in range(pieces)]
            others[step - 1].append(lax.ppermute(own[-1], "tp", source))
    parts = own + [part for group in others for part in group]
    place = lax.axis_index("tp").astype(jnp.int32).reshape(1)
    group = math.gcd(4, rows.shape[0] // len(parts))
    normed = norm_part(place, parts, norm_gain, pieces, group * rows.shape[2])
    return (jnp.concatenate(own, axis=1), attention_part(normed, rows))


def solution(mesh):
    placed = (
        P("ctx", None, "tp"),
        P(None, None, "tp"),
        P(None, "tp"),
        P(None, "tp"),
        P("tp"),
        P(),
        P("ctx", None, "tp"),
    )
    return jax.shard_map(
        on_device,
        mesh=mesh,
        in_specs=placed,
        out_specs=(P("ctx", "tp"), P("ctx", "tp")),
        check_vma=False,
    )
```
